512 devices in a mesh: line: 8 (over z), cable: 8 (over y), gate: 8 (over x, core).
Axes of the slice: x: 4, y: 8, z: 8, core: 2. Of those that a mesh axis runs over, the one named last changes fastest.
Arguments:
- recorded: bfloat16 [131072, 512], P(('cable', 'gate')), may hold values from -0.5 to 0.5
- trace_order: int32 [131072], replicated, may hold values from 0 to 131071, as said below
- shot_traces: bfloat16 [32, 128, 512], P('line', 'gate'), may hold values from -0.5 to 0.5
- line_picks: int32 [32, 128], P('line', 'gate'), may hold values from 0 to 2, as said below
- aperture_mask: int32 [1024, 128], P('cable', 'gate'), may hold values 0 or 1
Outputs:
- predicted: bfloat16 [512, 32, 1024], P('gate', 'line', 'cable')
The draws below stay inside these ranges and needn't reach their ends.
Inputs may be any that keep to these rules, and one draw needn't show every extreme that they name: `trace_order`: A permutation of 0 .. 131071; entry i names aperture point x and receiver r as x * 1024 + r. The owner of (x, r) is the device of cable r // 128 and gate x // 16. The 2048 entries of one aligned block of the list (those of one cable and gate device) name 64, 32 or 16 pairs of each owner, never more than 64, and exactly 64 for some owners. `line_picks`: value v at shot slot j of sail line l takes the shot of slot j on line l + v - 1; v is never 0 on the first line nor 2 on the last.
All inputs are finite; a program needn't handle non-finite values. No bound on the sum of `aperture_mask` on one device may be relied on, other than what follows from the above.
Results may differ from the reference program's by a relative error of at most 0.001.
Values may be sent and summed in bfloat16 or wider, within the bound.
No kernel may reach another device: no remote copies, remote signals or barrier semaphores. Data moves between devices by JAX's collectives and lax.ppermute only.
A program may use at most 64 MiB of HBM per device.

```python
import jax
import jax.numpy as jnp
import numpy as np
from jax import lax

NT = 512
SHOT_DEV = 4
REC_DEV = 128
APT_DEV = 16
SHOTS = 32
REC = 1024
APT = 128
TRACES = 131072
N_LINE = 8
N_CABLE = 8
N_GATE = 8


def draw_trace_order(key, part):
    key = jax.random.fold_in(key, 11)
    owners = N_CABLE * N_GATE
    per_dev = APT_DEV * REC_DEV
    mean_load = per_dev // owners
    receivers = REC_DEV * N_CABLE
    quarter = owners // 4
    base_loads = np.concatenate([np.full(quarter, 2 * mean_load), np.full(quarter, mean_load), np.full(owners - 2 * quarter, mean_load // 2)]).astype(np.int32)
    subkeys = jax.random.split(key, 4)
    pair_loads = jnp.asarray(base_loads)[jax.random.permutation(subkeys[0], owners)]
    position_of = jax.random.permutation(subkeys[1], owners)
    counts = pair_loads[(position_of[None, :] - position_of[:, None]) % owners]
    starts = jnp.cumsum(counts, axis=0) - counts
    row_perm = jax.vmap(lambda sub: jax.random.permutation(sub, per_dev))(jax.random.split(subkeys[2], owners))
    cum_ends = jnp.cumsum(counts, axis=1)
    slot_ids = jnp.arange(per_dev, dtype=jnp.int32)
    dest_owner = jnp.sum((cum_ends[:, None, :] <= slot_ids[None, :, None]).astype(jnp.int32), axis=2)
    source_ids = jnp.arange(owners, dtype=jnp.int32)[:, None]
    within = slot_ids[None, :] - (cum_ends - counts)[source_ids, dest_owner]
    local_row = row_perm[dest_owner, starts[source_ids, dest_owner] + within]
    cable_of = dest_owner // N_GATE
    gate_of = dest_owner % N_GATE
    aperture = gate_of * APT_DEV + local_row % APT_DEV
    receiver = cable_of * REC_DEV + local_row // APT_DEV
    flat_pairs = aperture * receivers + receiver
    shuffle = jax.vmap(lambda sub: jax.random.permutation(sub, per_dev))(jax.random.split(subkeys[3], owners))
    flat_pairs = jnp.take_along_axis(flat_pairs, shuffle, axis=1)
    return flat_pairs.reshape(-1).astype(jnp.int32)


def draw_line_picks(key, part):
    key = jax.random.fold_in(key, 23)
    pick_code = jax.random.randint(key, (SHOT_DEV * N_LINE, APT_DEV * N_GATE), 0, 3)
    line_of = (jnp.arange(SHOT_DEV * N_LINE) // SHOT_DEV)[:, None]
    pick_code = jnp.where(line_of == 0, jnp.maximum(pick_code, 1), pick_code)
    pick_code = jnp.where(line_of == N_LINE - 1, jnp.minimum(pick_code, 1), pick_code)
    return pick_code.astype(jnp.int32)


def plant(values, rng, smallest, largest):
    longest = values.shape.index(max(values.shape))
    spots = []
    for shift in (0, 1):
        where = [jax.random.randint(jax.random.fold_in(rng, axis), (), 0, length) for axis, length in enumerate(values.shape)]
        where[longest] = (where[longest] + shift) % values.shape[longest]
        spots.append(tuple(where))
    return values.at[spots[0]].set(smallest).at[spots[1]].set(largest)


def shard_levels(key, dims, cuts, smallest, top_value):
    level, own = 1.0, jax.random.fold_in(key, 6)
    for position, shards_of in cuts:
        draws = jnp.exp(jax.random.uniform(jax.random.fold_in(own, position), (shards_of,), jnp.float32, smallest / len(cuts), top_value / len(cuts)))
        level = level * jnp.repeat(draws, dims[position] // shards_of).reshape([-1 if axis == position else 1 for axis in range(len(dims))])
    return level


def scatter_about(rng, shape, scale, limit, shards=(), held_as=jnp.bfloat16):
    factor_of = shard_levels(rng, shape, shards, -0.22, 0.18) if shards else 1.0
    entries = jax.random.normal(rng, shape, jnp.float32) * scale * factor_of
    return jnp.minimum(jnp.maximum(entries, -limit), limit).astype(held_as)


def setup_inputs(seed: int = 0) -> dict:
    key_of = jax.random.split(jax.random.key(seed), 6)
    return {
        "recorded": scatter_about(key_of[0], (TRACES, NT), 0.08, 0.5, ((0, 64),)),
        "trace_order": draw_trace_order(jax.random.fold_in(key_of[5], 71), 0),
        "shot_traces": scatter_about(key_of[2], (SHOTS, APT, NT), 0.08, 0.5, ((0, 8), (1, 8))),
        "line_picks": draw_line_picks(jax.random.fold_in(key_of[5], 71), 0),
        "aperture_mask": plant((jax.random.randint(key_of[4], (REC, APT), 0, 4) < 3).astype(jnp.int32), jax.random.fold_in(key_of[4], 1), 0, 1),
    }


def reference(recorded, trace_order, shot_traces, line_picks, aperture_mask):
    aperture_count = APT_DEV * N_GATE
    receiver_count = REC_DEV * N_CABLE
    shot_count = SHOT_DEV * N_LINE
    gathers = jnp.zeros((aperture_count * receiver_count, NT), recorded.dtype).at[trace_order].set(recorded)
    gathers = gathers.reshape(aperture_count, receiver_count, NT)
    shot_rows = jnp.arange(shot_count, dtype=jnp.int32)[:, None] + (line_picks - 1) * SHOT_DEV
    aperture_cols = jnp.arange(aperture_count, dtype=jnp.int32)[None, :]
    near_traces = shot_traces[shot_rows, aperture_cols]
    lag_table = jnp.arange(NT, dtype=jnp.int32)[:, None] - jnp.arange(NT, dtype=jnp.int32)[None, :]
    causal = lag_table >= 0
    lag_index = jnp.maximum(lag_table, 0)

    def add_point(running, inputs):
        near_point, gather_point, mask_point = inputs
        toeplitz = jnp.where(causal[None], near_point.astype(jnp.float32)[:, lag_index], jnp.float32(0.0))
        weighted = gather_point.astype(jnp.float32) * mask_point.astype(jnp.float32)[:, None]
        return running + jnp.einsum("stk,rk->tsr", toeplitz, weighted), None

    initial = jnp.zeros((NT, shot_count, receiver_count), jnp.float32)
    final_sum, ignored = lax.scan(add_point, initial, (jnp.transpose(near_traces, (1, 0, 2)), gathers, aperture_mask.T))
    return final_sum.astype(jnp.bfloat16)
```

```python
import jax
import jax.numpy as jnp
from jax import lax
from jax.experimental import pallas as pl
from jax.experimental.pallas import tpu as pltpu
from jax.sharding import Mesh, PartitionSpec as P

NT = 512
LINES = 8
CABLES = 8
GATES = 8
CHIPS_X = 4
OWNERS = CABLES * GATES
PER_DEV = 2048
SHOT_DEV = 4
REC_DEV = 128
APT_DEV = 16
REC_BITS = 10
CAP = 64
HALF = CAP // 2
WIDTH = NT // LINES
LANES = 128
CHIPS = LINES * CHIPS_X
TAP = 16
TILE = 256

bf16 = jnp.bfloat16
f32 = jnp.float32
i32 = jnp.int32


def iota(shape, dim):
    return lax.broadcasted_iota(i32, shape, dim)


def params(**kw):
    return pltpu.CompilerParams(vmem_limit_bytes=56 * 1024 * 1024, **kw)


def owner_of(order):
    aperture = order >> REC_BITS
    receiver = order & ((1 << REC_BITS) - 1)
    return (receiver >> 7) * GATES + (aperture >> 4)


def earlier_matrix():
    return (iota((TILE, TILE), 0) < iota((TILE, TILE), 1)).astype(f32).astype(bf16)


def picked_rows(code_ref, source_ref, out_ref, finish):
    depth = source_ref.shape[0]
    rows = out_ref.shape[0]
    step = 1024

    def tile(m, carry):
        base = pl.multiple_of(m * TILE, TILE)
        total = jnp.zeros((TILE, LANES), f32)
        for c in range(depth // step):
            code = code_ref[:, c * step : (c + 1) * step] - base
            code = jnp.where((code >= 0) & (code < TILE), code, -1)
            code = code.astype(f32).astype(bf16)
            want = iota((TILE, step), 0).astype(f32).astype(bf16)
            onehot = jnp.where(want == code, bf16(1), bf16(0))
            total += jnp.dot(
                onehot, source_ref[c * step : (c + 1) * step, :], preferred_element_type=f32
            )
        out_ref[pl.ds(base, TILE), :] = finish(total, base).astype(out_ref.dtype)
        return carry

    lax.fori_loop(0, rows // TILE, tile, 0)


def send_kernel(where_ref, order_ref, rec_ref, out_ref, source, code):
    owner = owner_of(order_ref[...])
    before = earlier_matrix()
    carry = jnp.zeros((OWNERS, 1), f32)
    for c in range(PER_DEV // TILE):
        lanes = slice(c * TILE, (c + 1) * TILE)
        own = owner[:, lanes]
        onehot = jnp.where(iota((OWNERS, TILE), 0) == own, 1.0, 0.0).astype(f32)
        count = jnp.dot(onehot.astype(bf16), before, preferred_element_type=f32) + carry
        rank = jnp.sum(onehot * count, axis=0, keepdims=True).astype(i32)
        carry = carry + jnp.sum(onehot, axis=1, keepdims=True)
        slot = own * HALF + rank
        code[:, c * TILE : (c + 1) * TILE] = jnp.where(rank < HALF, slot, -1)
        code[:, PER_DEV + c * TILE : PER_DEV + (c + 1) * TILE] = jnp.where(
            rank >= HALF, slot - HALF, -1
        )
    odd = where_ref[1] == 1
    for c in range(PER_DEV // TILE):
        rows = slice(c * TILE, (c + 1) * TILE)
        here = rec_ref[rows, :].astype(f32)
        turned = pltpu.roll(here, WIDTH, 1)
        low = iota((TILE, LANES), 1) < WIDTH
        source[rows, :] = jnp.where(low, jnp.where(odd, turned, here), 0.0).astype(bf16)
        source[PER_DEV + c * TILE : PER_DEV + (c + 1) * TILE, :] = jnp.where(
            low, 0.0, jnp.where(odd, here, turned)
        ).astype(bf16)
    picked_rows(code, source, out_ref, lambda total, base: total)


def send(recorded, my_order, where):
    return pl.pallas_call(
        send_kernel,
        out_shape=jax.ShapeDtypeStruct((OWNERS * HALF, LANES), bf16),
        grid_spec=pltpu.PrefetchScalarGridSpec(
            num_scalar_prefetch=1,
            grid=(1,),
            in_specs=[
                pl.BlockSpec((1, PER_DEV), lambda i, w: (0, 0)),
                pl.BlockSpec((PER_DEV, LANES), lambda i, w: (0, w[0])),
            ],
            out_specs=pl.BlockSpec((OWNERS * HALF, LANES), lambda i, w: (0, 0)),
            scratch_shapes=[
                pltpu.VMEM((2 * PER_DEV, LANES), bf16),
                pltpu.VMEM((1, 2 * PER_DEV), i32),
            ],
        ),
        compiler_params=params(),
        name="send_rows",
    )(where, my_order, recorded)


def place_kernel(me_ref, order_ref, out_ref, key, chip_ref, row_ref):
    me = me_ref[0]
    before = earlier_matrix()
    carry = jnp.zeros((OWNERS, 1), f32)
    for c in range(PER_DEV // TILE):
        lanes = slice(c * TILE, (c + 1) * TILE)
        order = order_ref[:, lanes]
        mine = jnp.where(owner_of(order) == me, 1.0, 0.0).astype(f32)
        count = jnp.dot(mine.astype(bf16), before, preferred_element_type=f32) + carry
        carry = carry + jnp.sum(mine, axis=1, keepdims=True)
        key[:, lanes] = jnp.where(mine > 0.5, count, -1.0)
        receiver = order & (REC_DEV - 1)
        chip_ref[:, lanes] = (receiver & (CHIPS - 1)).astype(f32)
        row_ref[:, lanes] = ((receiver >> 5) * APT_DEV + ((order >> REC_BITS) & 15)).astype(f32)

    def group(g, carry):
        eight = pl.ds(pl.multiple_of(g * 8, 8), 8)
        all_keys = key[eight, :]
        chips = chip_ref[eight, :]
        local_rows = row_ref[eight, :]
        ones = jnp.ones((4, PER_DEV), f32)
        want = iota((HALF, PER_DEV), 0)
        for part in range(2):
            four = slice(4 * part, 4 * part + 4)
            values = jnp.concatenate([chips[four], local_rows[four], ones, 0 * ones], axis=0)
            values = values.astype(bf16)
            blocks = []
            for half in range(2):
                wanted = (want + half * HALF).astype(f32).astype(bf16)
                for b in range(4):
                    mine = all_keys[4 * part + b : 4 * part + b + 1].astype(bf16)
                    blocks.append(jnp.where(wanted == mine, bf16(1), bf16(0)))
            onehot = jnp.concatenate(blocks, axis=0)
            found = lax.dot_general(
                values, onehot, (((1,), (1,)), ((), ())), preferred_element_type=f32
            )
            own = (iota((16, TILE), 0) & 3) == ((iota((16, TILE), 1) & (LANES - 1)) >> 5)
            found = jnp.where(own, found, 0.0)
            chip = jnp.sum(found[0:4], axis=0, keepdims=True).astype(i32)
            row = jnp.sum(found[4:8], axis=0, keepdims=True).astype(i32)
            valid = jnp.sum(found[8:12], axis=0, keepdims=True) > 0.5
            code = chip * 32 + (row & 31)
            at = pl.ds(pl.multiple_of((2 * g + part) * LANES, LANES), LANES)
            for upper in range(2):
                placed = jnp.where(valid & ((row >> 5) == upper), code, -1)
                for half in range(2):
                    out_ref[2 * upper + half : 2 * upper + half + 1, at] = placed[
                        :, half * LANES : (half + 1) * LANES
                    ]
        return carry

    lax.fori_loop(0, OWNERS // 8, group, 0)


def place(orders, me):
    return pl.pallas_call(
        place_kernel,
        out_shape=jax.ShapeDtypeStruct((4, OWNERS * HALF), i32),
        in_specs=[
            pl.BlockSpec(memory_space=pltpu.SMEM),
            pl.BlockSpec(memory_space=pltpu.VMEM),
        ],
        out_specs=pl.BlockSpec(memory_space=pltpu.VMEM),
        scratch_shapes=[pltpu.VMEM((OWNERS, PER_DEV), f32)] * 3,
        compiler_params=params(),
        cost_estimate=pl.CostEstimate(
            flops=4 * 2**30, bytes_accessed=2**20, transcendentals=0
        ),
        name="place_rows",
    )(me, orders)


def receive_kernel(key_ref, got_ref, mask_ref, out_ref, source, code):
    for v in range(4):
        code[:, v * PER_DEV : (v + 1) * PER_DEV] = key_ref[v : v + 1, :]
    for c in range(PER_DEV // TILE):
        rows = slice(c * TILE, (c + 1) * TILE)
        here = got_ref[rows, :].astype(f32)
        turned = pltpu.roll(here, WIDTH, 1)
        low = iota((TILE, LANES), 1) < WIDTH
        parts = (
            jnp.where(low, here, 0.0),
            jnp.where(low, turned, 0.0),
            jnp.where(low, 0.0, turned),
            jnp.where(low, 0.0, here),
        )
        for v, part in enumerate(parts):
            source[v * PER_DEV + c * TILE : v * PER_DEV + (c + 1) * TILE, :] = part.astype(bf16)

    def weighted(total, base):
        return total * mask_ref[pl.ds(base, TILE), :].astype(f32)

    picked_rows(code, source, out_ref, weighted)


def receive(keys, got, weights):
    return pl.pallas_call(
        receive_kernel,
        out_shape=jax.ShapeDtypeStruct((CHIPS * 32, LANES), bf16),
        in_specs=[pl.BlockSpec(memory_space=pltpu.VMEM)] * 3,
        out_specs=pl.BlockSpec(memory_space=pltpu.VMEM),
        scratch_shapes=[
            pltpu.VMEM((4 * PER_DEV, LANES), bf16),
            pltpu.VMEM((1, 4 * PER_DEV), i32),
        ],
        compiler_params=params(),
        name="receive_rows",
    )(keys, got, weights)


def near_kernel(all_ref, near_ref):
    def one_line(line, carry):
        before = jnp.maximum(line - 1, 0)
        after = jnp.minimum(line + 1, LINES - 1)
        for gx in range(CHIPS_X):
            pick = all_ref[line, gx, 128:144, :]
            for g in range(8):
                rows = slice(g * 16, (g + 1) * 16)
                near_ref[line, rows, gx * 256 : (gx + 1) * 256] = jnp.where(
                    pick == bf16(0),
                    all_ref[before, gx, rows, :],
                    jnp.where(
                        pick == bf16(1), all_ref[line, gx, rows, :], all_ref[after, gx, rows, :]
                    ),
                )
        return carry

    lax.fori_loop(0, LINES, one_line, 0)


def near(everyone):
    return pl.pallas_call(
        near_kernel,
        out_shape=jax.ShapeDtypeStruct((LINES, 128, CHIPS_X * 256), bf16),
        in_specs=[pl.BlockSpec(memory_space=pltpu.VMEM)],
        out_specs=pl.BlockSpec(memory_space=pltpu.VMEM),
        compiler_params=params(),
        name="near_rows",
    )(everyone)


def predict_kernel(gather_ref, near_ref, out_ref, base, lagged, total):
    low = iota((APT_DEV, LANES), 1) < WIDTH
    lane = iota((TAP, LANES), 1)
    tap = iota((TAP, LANES), 0)

    def one_block(n, carry):
        gx = n // 2
        rho = n % 2
        for c in range(4):
            even = gather_ref[2 * c * CHIPS_X + gx, pl.ds(rho * 16, 16), :].astype(f32)
            odd = gather_ref[(2 * c + 1) * CHIPS_X + gx, pl.ds(rho * 16, 16), :].astype(f32)
            base[0, :, c * LANES : (c + 1) * LANES] = jnp.where(
                low, even, pltpu.roll(odd, WIDTH, 1)
            )
            base[1, :, c * LANES : (c + 1) * LANES] = jnp.where(
                low, pltpu.roll(even, WIDTH, 1), odd
            )
        for upper in range(2):
            lanes = pl.ds(pl.multiple_of((2 * upper + rho) * LANES, LANES), LANES)
            for x in range(APT_DEV):
                rows = pl.ds(pl.multiple_of((gx * APT_DEV + x) * TAP, TAP), TAP)
                last = jnp.zeros((TAP, LANES), f32)
                for c in range(4):
                    row = base[upper, x : x + 1, c * LANES : (c + 1) * LANES]
                    row = jnp.broadcast_to(row, (TAP, LANES))
                    turned = pltpu.roll(row, 0, 1, stride=1, stride_axis=0)
                    lagged[c, rows, lanes] = jnp.where(lane >= tap, turned, last).astype(bf16)
                    last = turned
        return carry

    lax.fori_loop(0, 2 * CHIPS_X, one_block, 0)

    second = iota((8, LANES), 0) >> 2
    lane8 = iota((8, LANES), 1)
    half8 = lane8 < WIDTH

    def one_line(line, carry):
        for d in range(4):
            part = jnp.dot(
                near_ref[line, 0 : 128 - 32 * d, :], lagged[d], preferred_element_type=f32
            )
            if d == 0:
                total[...] = part
            else:
                total[32 * d :, :] += part
        spill = [jnp.zeros((8, LANES), f32)] * 4
        for i in range(4):
            parts = []
            for rho in range(4):
                current = spill[rho]
                later = jnp.zeros((8, LANES), f32)
                for q in range(4):
                    rows = slice(32 * i + 8 * q, 32 * i + 8 * q + 8)
                    piece = total[rows, rho * LANES : (rho + 1) * LANES]
                    first = piece if q == 0 else pltpu.roll(piece, 32 * q, 1)
                    turned = jnp.where(
                        second == 0, first, pltpu.roll(piece, 32 * q + TAP, 1)
                    )
                    stays = lane8 >= 32 * q + TAP * second
                    current = current + jnp.where(stays, turned, 0.0)
                    later = later + jnp.where(stays, 0.0, turned)
                spill[rho] = later
                parts.append(current[0:4] + current[4:8])
            for k in range(2):
                for rho in range(2):
                    one, two = parts[rho], parts[2 + rho]
                    if k == 0:
                        packed = jnp.where(half8[0:4], one, pltpu.roll(two, WIDTH, 1))
                    else:
                        packed = jnp.where(half8[0:4], pltpu.roll(one, WIDTH, 1), two)
                    out_ref[line * GATES + 2 * i + k, 4 * rho : 4 * rho + 4, :] = packed
        return carry

    lax.fori_loop(0, LINES, one_line, 0)


def predict(gathers, near_all):
    return pl.pallas_call(
        predict_kernel,
        out_shape=jax.ShapeDtypeStruct((OWNERS, 8, LANES), f32),
        in_specs=[pl.BlockSpec(memory_space=pltpu.VMEM)] * 2,
        out_specs=pl.BlockSpec(memory_space=pltpu.VMEM),
        scratch_shapes=[
            pltpu.VMEM((2, APT_DEV, NT), f32),
            pltpu.VMEM((4, CHIPS_X * APT_DEV * TAP, 4 * LANES), bf16),
            pltpu.VMEM((128, 4 * LANES), f32),
        ],
        compiler_params=params(),
        name="predict_part",
    )(gathers, near_all)


def finish_kernel(parts_ref, out_ref):
    shots = []
    for s in range(SHOT_DEV):
        rows = []
        for rho in range(2):
            both = parts_ref[:, 0, 4 * rho + s, :] + parts_ref[:, 1, 4 * rho + s, :]
            rows.append(both)
        turned = jnp.transpose(jnp.concatenate(rows, axis=0))
        shots.append(jnp.concatenate([turned[:WIDTH], turned[WIDTH:]], axis=1))
    out_ref[...] = jnp.stack(shots, axis=1).astype(out_ref.dtype)


def finish(parts):
    return pl.pallas_call(
        finish_kernel,
        out_shape=jax.ShapeDtypeStruct((NT // GATES, SHOT_DEV, REC_DEV), bf16),
        in_specs=[pl.BlockSpec(memory_space=pltpu.VMEM)],
        out_specs=pl.BlockSpec(memory_space=pltpu.VMEM),
        compiler_params=params(),
        name="finish_sum",
    )(parts)


def on_device(recorded, trace_order, shot_traces, line_picks, aperture_mask):
    gate = ("gx", "core")
    me = lax.axis_index(("cable",) + gate).astype(i32)
    line = lax.axis_index("line").astype(i32)

    shots = shot_traces.reshape(SHOT_DEV, APT_DEV, NT // TAP, TAP)
    shots = jnp.transpose(shots, (2, 0, 1, 3)).reshape(NT // TAP * SHOT_DEV, APT_DEV * TAP)
    picks = jnp.tile(jnp.repeat(line_picks, TAP, axis=1), (4, 1)).astype(bf16)
    everyone = lax.all_gather(
        jnp.concatenate([shots, picks], axis=0), ("line", "gx"), axis=0, tiled=True
    )

    my_order = lax.dynamic_slice_in_dim(trace_order, me * PER_DEV, PER_DEV).reshape(1, PER_DEV)
    outgoing = send(recorded, my_order, jnp.stack([line // 2, line % 2]))
    got = lax.all_to_all(
        outgoing.reshape(OWNERS, HALF, LANES),
        ("cable",) + gate,
        split_axis=0,
        concat_axis=0,
        tiled=True,
    )
    keys = place(trace_order.reshape(OWNERS, PER_DEV), me.reshape(1))
    weights = aperture_mask.astype(bf16).reshape(2, 2, CHIPS, APT_DEV)
    weights = jnp.transpose(weights, (2, 1, 3, 0)).reshape(CHIPS * 32, 2)
    weights = jnp.repeat(weights, WIDTH, axis=1)
    mine = receive(keys, got.reshape(OWNERS * HALF, LANES), weights)
    gathers = lax.all_to_all(
        mine.reshape(CHIPS, 32, LANES), ("line", "gx"), split_axis=0, concat_axis=0, tiled=True
    )
    near_all = near(everyone.reshape(LINES, CHIPS_X, 144, 256))
    part = predict(gathers, near_all)
    parts = lax.all_to_all(part, ("line",) + gate, split_axis=0, concat_axis=0, tiled=True)
    return finish(parts.reshape(CHIPS, 2, 8, LANES))


def solution(mesh):
    split = Mesh(mesh.devices.reshape(LINES, CABLES, CHIPS_X, 2), ("line", "cable", "gx", "core"))
    gate = ("gx", "core")
    placed = (
        P(("cable",) + gate, None),
        P(),
        P("line", gate, None),
        P("line", gate),
        P("cable", gate),
    )
    return jax.shard_map(
        on_device,
        mesh=split,
        in_specs=placed,
        out_specs=P(gate, "line", "cable"),
        check_vma=False,
    )
```

```python
import jax
import jax.numpy as jnp
from jax import lax
from jax.experimental import pallas as pl
from jax.experimental.pallas import tpu as pltpu
from jax.sharding import Mesh, PartitionSpec as P

NT = 512
LINES = 8
CABLES = 8
GATES = 8
CHIPS_X = 4
OWNERS = CABLES * GATES
PER_DEV = 2048
SHOT_DEV = 4
REC_DEV = 128
APT_DEV = 16
REC_BITS = 10
CAP = 64
HALF = CAP // 2
WIDTH = NT // LINES
LANES = 128
SHARES = LINES * 2
UPPER = 4
TAP = 16
TILE = 256
MOVED = 1024

bf16 = jnp.bfloat16
f32 = jnp.float32
i32 = jnp.int32


def iota(shape, dim):
    return lax.broadcasted_iota(i32, shape, dim)


def params(mib):
    return pltpu.CompilerParams(vmem_limit_bytes=mib * 1024 * 1024)


def owner_of(order):
    aperture = order >> REC_BITS
    receiver = order & ((1 << REC_BITS) - 1)
    return (receiver >> 7) * GATES + (aperture >> 4)


def earlier_matrix():
    return (iota((TILE, TILE), 0) < iota((TILE, TILE), 1)).astype(f32).astype(bf16)


def picked_rows(code_ref, source_ref, out_ref, finish):
    depth = source_ref.shape[0]
    rows = out_ref.shape[0]
    want = iota((TILE, TILE), 0).astype(f32).astype(bf16)

    def tile(m, carry):
        base = pl.multiple_of(m * MOVED, MOVED)
        total = jnp.zeros((MOVED, LANES), f32)
        for c in range(depth // TILE):
            at = slice(c * TILE, (c + 1) * TILE)
            blocks = []
            for b in range(MOVED // TILE):
                code = code_ref[:, at] - (base + b * TILE)
                code = jnp.where((code >= 0) & (code < TILE), code, -1)
                code = code.astype(f32).astype(bf16)
                blocks.append(jnp.where(want == code, bf16(1), bf16(0)))
            total += jnp.dot(
                jnp.concatenate(blocks, axis=0), source_ref[at, :], preferred_element_type=f32
            )
        out_ref[pl.ds(base, MOVED), :] = finish(total, base).astype(out_ref.dtype)
        return carry

    lax.fori_loop(0, rows // MOVED, tile, 0)


def send_kernel(where_ref, order_hbm, rec_hbm, out_ref, order_ref, rec_ref, source, code, sems):
    line, me = where_ref[0], where_ref[1]
    order_copy = pltpu.make_async_copy(
        order_hbm.at[pl.ds(pl.multiple_of(me * PER_DEV, PER_DEV), PER_DEV)], order_ref, sems.at[0]
    )
    rec_copy = pltpu.make_async_copy(
        rec_hbm.at[:, pl.ds(pl.multiple_of((line >> 1) * LANES, LANES), LANES)],
        rec_ref,
        sems.at[1],
    )
    order_copy.start()
    rec_copy.start()
    order_copy.wait()
    owner = owner_of(order_ref[...].reshape(1, PER_DEV))
    before = earlier_matrix()
    carry = jnp.zeros((OWNERS, 1), f32)
    for c in range(PER_DEV // TILE):
        lanes = slice(c * TILE, (c + 1) * TILE)
        own = owner[:, lanes]
        onehot = jnp.where(iota((OWNERS, TILE), 0) == own, 1.0, 0.0).astype(f32)
        count = jnp.dot(onehot.astype(bf16), before, preferred_element_type=f32) + carry
        rank = jnp.sum(onehot * count, axis=0, keepdims=True).astype(i32)
        carry = carry + jnp.sum(onehot, axis=1, keepdims=True)
        slot = own * HALF + rank
        code[:, c * TILE : (c + 1) * TILE] = jnp.where(rank < HALF, slot, -1)
        code[:, PER_DEV + c * TILE : PER_DEV + (c + 1) * TILE] = jnp.where(
            rank >= HALF, slot - HALF, -1
        )
    rec_copy.wait()
    odd = line & 1 == 1
    for c in range(PER_DEV // TILE):
        rows = slice(c * TILE, (c + 1) * TILE)
        here = rec_ref[rows, :].astype(f32)
        turned = pltpu.roll(here, WIDTH, 1)
        low = iota((TILE, LANES), 1) < WIDTH
        source[rows, :] = jnp.where(low, jnp.where(odd, turned, here), 0.0).astype(bf16)
        source[PER_DEV + c * TILE : PER_DEV + (c + 1) * TILE, :] = jnp.where(
            low, 0.0, jnp.where(odd, here, turned)
        ).astype(bf16)
    picked_rows(code, source, out_ref, lambda total, base: total)


def send(recorded, trace_order, where):
    return pl.pallas_call(
        send_kernel,
        out_shape=jax.ShapeDtypeStruct((OWNERS * HALF, LANES), bf16),
        in_specs=[
            pl.BlockSpec(memory_space=pltpu.SMEM),
            pl.BlockSpec(memory_space=pltpu.HBM),
            pl.BlockSpec(memory_space=pltpu.HBM),
        ],
        out_specs=pl.BlockSpec(memory_space=pltpu.VMEM),
        scratch_shapes=[
            pltpu.VMEM((PER_DEV,), i32),
            pltpu.VMEM((PER_DEV, LANES), bf16),
            pltpu.VMEM((2 * PER_DEV, LANES), bf16),
            pltpu.VMEM((1, 2 * PER_DEV), i32),
            pltpu.SemaphoreType.DMA((2,)),
        ],
        compiler_params=params(58),
        name="send_rows",
    )(where, trace_order, recorded)


def place_kernel(me_ref, order_ref, out_ref, key, chip_ref, row_ref):
    me = me_ref[0]
    before = earlier_matrix()
    carry = jnp.zeros((OWNERS, 1), f32)
    for c in range(PER_DEV // TILE):
        lanes = slice(c * TILE, (c + 1) * TILE)
        order = order_ref[:, lanes]
        mine = jnp.where(owner_of(order) == me, 1.0, 0.0).astype(f32)
        count = jnp.dot(mine.astype(bf16), before, preferred_element_type=f32) + carry
        carry = carry + jnp.sum(mine, axis=1, keepdims=True)
        key[:, lanes] = jnp.where(mine > 0.5, count, -1.0)
        receiver = order & (REC_DEV - 1)
        chip_ref[:, lanes] = (receiver & (SHARES - 1)).astype(f32)
        row_ref[:, lanes] = ((receiver >> 4) * APT_DEV + ((order >> REC_BITS) & 15)).astype(f32)

    def group(g, carry):
        eight = pl.ds(pl.multiple_of(g * 8, 8), 8)
        all_keys = key[eight, :]
        chips = chip_ref[eight, :]
        local_rows = row_ref[eight, :]
        ones = jnp.ones((4, PER_DEV), f32)
        want = iota((HALF, PER_DEV), 0)
        for part in range(2):
            four = slice(4 * part, 4 * part + 4)
            values = jnp.concatenate([chips[four], local_rows[four], ones, 0 * ones], axis=0)
            values = values.astype(bf16)
            blocks = []
            for half in range(2):
                wanted = (want + half * HALF).astype(f32).astype(bf16)
                for b in range(4):
                    mine = all_keys[4 * part + b : 4 * part + b + 1].astype(bf16)
                    blocks.append(jnp.where(wanted == mine, bf16(1), bf16(0)))
            onehot = jnp.concatenate(blocks, axis=0)
            found = lax.dot_general(
                values, onehot, (((1,), (1,)), ((), ())), preferred_element_type=f32
            )
            own = (iota((16, TILE), 0) & 3) == ((iota((16, TILE), 1) & (LANES - 1)) >> 5)
            found = jnp.where(own, found, 0.0)
            chip = jnp.sum(found[0:4], axis=0, keepdims=True).astype(i32)
            row = jnp.sum(found[4:8], axis=0, keepdims=True).astype(i32)
            valid = jnp.sum(found[8:12], axis=0, keepdims=True) > 0.5
            code = chip * 64 + (row & 63)
            at = pl.ds(pl.multiple_of((2 * g + part) * LANES, LANES), LANES)
            for upper in range(2):
                placed = jnp.where(valid & ((row >> 6) == upper), code, -1)
                for half in range(2):
                    out_ref[2 * upper + half : 2 * upper + half + 1, at] = placed[
                        :, half * LANES : (half + 1) * LANES
                    ]
        return carry

    lax.fori_loop(0, OWNERS // 8, group, 0)


def place(orders, me):
    return pl.pallas_call(
        place_kernel,
        out_shape=jax.ShapeDtypeStruct((4, OWNERS * HALF), i32),
        in_specs=[
            pl.BlockSpec(memory_space=pltpu.SMEM),
            pl.BlockSpec(memory_space=pltpu.VMEM),
        ],
        out_specs=pl.BlockSpec(memory_space=pltpu.VMEM),
        scratch_shapes=[pltpu.VMEM((OWNERS, PER_DEV), f32)] * 3,
        compiler_params=params(12),
        cost_estimate=pl.CostEstimate(
            flops=4 * 2**30, bytes_accessed=2**20, transcendentals=0
        ),
        name="place_rows",
    )(me, orders)


def receive_kernel(key_ref, got_ref, mask_ref, out_ref, source, code):
    for v in range(4):
        code[:, v * PER_DEV : (v + 1) * PER_DEV] = key_ref[v : v + 1, :]
    for c in range(PER_DEV // TILE):
        rows = slice(c * TILE, (c + 1) * TILE)
        here = got_ref[rows, :].astype(f32)
        turned = pltpu.roll(here, WIDTH, 1)
        low = iota((TILE, LANES), 1) < WIDTH
        parts = (
            jnp.where(low, here, 0.0),
            jnp.where(low, turned, 0.0),
            jnp.where(low, 0.0, turned),
            jnp.where(low, 0.0, here),
        )
        for v, part in enumerate(parts):
            source[v * PER_DEV + c * TILE : v * PER_DEV + (c + 1) * TILE, :] = part.astype(bf16)

    def weighted(total, base):
        return total * mask_ref[pl.ds(base, MOVED), :].astype(f32)

    picked_rows(code, source, out_ref, weighted)


def receive(keys, got, weights):
    return pl.pallas_call(
        receive_kernel,
        out_shape=jax.ShapeDtypeStruct((SHARES * 64, LANES), bf16),
        in_specs=[pl.BlockSpec(memory_space=pltpu.VMEM)] * 3,
        out_specs=pl.BlockSpec(memory_space=pltpu.VMEM),
        scratch_shapes=[
            pltpu.VMEM((4 * PER_DEV, LANES), bf16),
            pltpu.VMEM((1, 4 * PER_DEV), i32),
        ],
        compiler_params=params(12),
        name="receive_rows",
    )(keys, got, weights)


def near_kernel(where_ref, own_ref, other_ref, near_ref):
    me, core = where_ref[0], where_ref[1]

    def held(line):
        offset = line ^ me
        return ((offset & 1) << 2) | (offset & 2) | (offset >> 2)

    def one_line(line, carry):
        here = held(line)
        before = held(jnp.maximum(line - 1, 0))
        after = held(jnp.minimum(line + 1, LINES - 1))
        for side, all_ref in enumerate((own_ref, other_ref)):
            at = pl.multiple_of((core ^ side) * 256, 256)
            pick = all_ref[here, 128:144, :]
            first, own = pick == bf16(0), pick == bf16(1)
            for g in range(8):
                rows = slice(g * 16, (g + 1) * 16)
                near_ref[line, rows, pl.ds(at, 256)] = jnp.where(
                    first,
                    all_ref[before, rows, :],
                    jnp.where(own, all_ref[here, rows, :], all_ref[after, rows, :]),
                )
        return carry

    lax.fori_loop(0, LINES, one_line, 0)


def near(where, own, other):
    return pl.pallas_call(
        near_kernel,
        out_shape=jax.ShapeDtypeStruct((LINES, 128, 512), bf16),
        in_specs=[
            pl.BlockSpec(memory_space=pltpu.SMEM),
            pl.BlockSpec(memory_space=pltpu.VMEM),
            pl.BlockSpec(memory_space=pltpu.VMEM),
        ],
        out_specs=pl.BlockSpec(memory_space=pltpu.VMEM),
        compiler_params=params(8),
        name="near_rows",
    )(where, own, other)


def swapped(held, axis, bit):
    size = lax.axis_size(axis)
    return lax.ppermute(held, axis, [(i, i ^ bit) for i in range(size)])


def lag_rows(gather_ref, base, lagged):
    low = iota((APT_DEV, LANES), 1) < WIDTH
    lane = iota((TAP, LANES), 1)
    tap = iota((TAP, LANES), 0)

    def one_block(n, carry):
        core = n // UPPER
        rho = n % UPPER
        for c in range(4):
            rows = pl.ds(pl.multiple_of(rho * 16, 16), 16)
            even = gather_ref[4 * c + core, rows, :].astype(f32)
            odd = gather_ref[4 * c + 2 + core, rows, :].astype(f32)
            base[0, :, c * LANES : (c + 1) * LANES] = jnp.where(
                low, even, pltpu.roll(odd, WIDTH, 1)
            )
            base[1, :, c * LANES : (c + 1) * LANES] = jnp.where(
                low, pltpu.roll(even, WIDTH, 1), odd
            )
        for upper in range(2):
            lanes = pl.ds(pl.multiple_of((2 * rho + upper) * LANES, LANES), LANES)
            for x in range(APT_DEV):
                rows = pl.ds(pl.multiple_of((core * APT_DEV + x) * TAP, TAP), TAP)
                last = jnp.zeros((TAP, LANES), f32)
                for c in range(4):
                    row = base[upper, x : x + 1, c * LANES : (c + 1) * LANES]
                    row = jnp.broadcast_to(row, (TAP, LANES))
                    turned = pltpu.roll(row, 0, 1, stride=1, stride_axis=0)
                    lagged[c, rows, lanes] = jnp.where(lane >= tap, turned, last).astype(bf16)
                    last = turned
        return carry

    lax.fori_loop(0, 2 * UPPER, one_block, 0)


def sum_lines(near_ref, lagged, out_ref):
    lane = iota((8 * LINES, LANES), 1)
    low = lane < WIDTH

    for rho in range(UPPER):
        spill = [jnp.zeros((8 * LINES, LANES), f32)] * 2
        before = [jnp.zeros((8 * LINES, LANES), f32)] * 2
        for i in range(4):
            total = None
            for d in range(i + 1):
                here = near_ref[:, 32 * (i - d) : 32 * (i - d) + 32, :].reshape(32 * LINES, 512)
                part = jnp.dot(
                    here, lagged[d, :, 256 * rho : 256 * rho + 256], preferred_element_type=f32
                )
                total = part if total is None else total + part
            total = total.reshape(LINES, 4, 8, 256)
            done = []
            for upper in range(2):
                current = spill[upper]
                later = jnp.zeros((8 * LINES, LANES), f32)
                for q in range(4):
                    piece = total[:, q, :, upper * LANES : (upper + 1) * LANES]
                    piece = piece.reshape(8 * LINES, LANES)
                    if q == 0:
                        current = current + piece
                    else:
                        turned = pltpu.roll(piece, 32 * q, 1)
                        current = current + jnp.where(lane >= 32 * q, turned, 0.0)
                        later = later + jnp.where(lane >= 32 * q, 0.0, turned)
                turned = pltpu.roll(current, TAP, 1)
                moved = jnp.where(lane >= TAP, turned, before[upper])
                spill[upper] = later
                before[upper] = turned
                both = current.reshape(LINES, 8, LANES)[:, 0:4] + moved.reshape(LINES, 8, LANES)[:, 4:8]
                done.append(both.reshape(4 * LINES, LANES))
            one, two = done
            half = low[: 4 * LINES]
            rows = slice(4 * rho, 4 * rho + 4)
            even = jnp.where(half, one, pltpu.roll(two, WIDTH, 1)).reshape(LINES, 4, LANES)
            odd = jnp.where(half, pltpu.roll(one, WIDTH, 1), two).reshape(LINES, 4, LANES)
            out_ref[:, 2 * i, rows, :] = even
            out_ref[:, 2 * i + 1, rows, :] = odd


def predict_kernel(gather_ref, near_ref, out_ref, base, lagged):
    lag_rows(gather_ref, base, lagged)
    sum_lines(near_ref, lagged, out_ref)


def predict(gathers, near_all):
    return pl.pallas_call(
        predict_kernel,
        out_shape=jax.ShapeDtypeStruct((LINES, GATES, 4 * UPPER, LANES), f32),
        in_specs=[pl.BlockSpec(memory_space=pltpu.VMEM)] * 2,
        out_specs=pl.BlockSpec(memory_space=pltpu.VMEM),
        scratch_shapes=[
            pltpu.VMEM((2, APT_DEV, NT), f32),
            pltpu.VMEM((4, 2 * APT_DEV * TAP, 2 * UPPER * LANES), bf16),
        ],
        compiler_params=params(20),
        name="predict_part",
    )(gathers, near_all)


def finish_kernel(parts_ref, out_ref):
    total = jnp.sum(parts_ref[...], axis=1).reshape(SHARES, 4 * UPPER, LANES)
    shots = []
    for s in range(SHOT_DEV):
        rows = []
        for rho in range(UPPER):
            rows.append(total[:, 4 * rho + s, :])
        turned = jnp.transpose(jnp.concatenate(rows, axis=0))
        shots.append(jnp.concatenate([turned[:WIDTH], turned[WIDTH:]], axis=1))
    out_ref[...] = jnp.stack(shots, axis=1).astype(out_ref.dtype)


def finish(parts):
    return pl.pallas_call(
        finish_kernel,
        out_shape=jax.ShapeDtypeStruct((NT // GATES, SHOT_DEV, REC_DEV), bf16),
        in_specs=[pl.BlockSpec(memory_space=pltpu.VMEM)],
        out_specs=pl.BlockSpec(memory_space=pltpu.VMEM),
        compiler_params=params(6),
        name="finish_sum",
    )(parts)


def on_device(recorded, trace_order, shot_traces, line_picks, aperture_mask):
    gate = ("gx", "core")
    me = lax.axis_index(("cable",) + gate).astype(i32)
    line = lax.axis_index("line").astype(i32)

    shots = shot_traces.reshape(SHOT_DEV, APT_DEV, NT // TAP, TAP)
    shots = jnp.transpose(shots, (2, 0, 1, 3)).reshape(NT // TAP * SHOT_DEV, APT_DEV * TAP)
    picks = jnp.tile(jnp.repeat(line_picks, TAP, axis=1), (4, 1)).astype(bf16)
    held = jnp.concatenate([shots, picks], axis=0)[None]
    four = swapped(held, "line", 4)

    outgoing = send(recorded, trace_order, jnp.stack([line, me]))
    got = lax.all_to_all(
        outgoing.reshape(OWNERS, HALF, LANES),
        ("cable",) + gate,
        split_axis=0,
        concat_axis=0,
        tiled=True,
    )
    late, four, trace_order, aperture_mask = lax.optimization_barrier(
        (outgoing, four, trace_order, aperture_mask)
    )
    held = jnp.concatenate([held, four], axis=0)
    two = swapped(held, "line", 2)
    keys = place(trace_order.reshape(OWNERS, PER_DEV), me.reshape(1))
    keys, two = lax.optimization_barrier((keys, two))
    held = jnp.concatenate([held, two], axis=0)
    one = swapped(held, "line", 1)
    weights = aperture_mask.astype(bf16).reshape(2, UPPER, SHARES, APT_DEV)
    weights = jnp.transpose(weights, (2, 1, 3, 0)).reshape(SHARES * 64, 2)
    weights = jnp.repeat(weights, WIDTH, axis=1)
    mine = receive(keys, got.reshape(OWNERS * HALF, LANES), weights)
    gathers = lax.all_to_all(
        mine.reshape(SHARES, 64, LANES), ("line", "core"), split_axis=0, concat_axis=0, tiled=True
    )
    late, one = lax.optimization_barrier((mine, one))
    own = jnp.concatenate([held, one], axis=0)
    other = swapped(own, "core", 1)
    near_all = near(jnp.stack([line, lax.axis_index("core").astype(i32)]), own, other)
    part = predict(gathers, near_all)
    parts = lax.all_to_all(
        part.reshape(OWNERS, 4 * UPPER, LANES), ("line",) + gate, split_axis=0, concat_axis=0, tiled=True)
    return finish(parts.reshape(LINES, CHIPS_X, 2, 4 * UPPER, LANES))


def solution(mesh):
    split = Mesh(mesh.devices.reshape(LINES, CABLES, CHIPS_X, 2), ("line", "cable", "gx", "core"))
    gate = ("gx", "core")
    placed = (
        P(("cable",) + gate, None),
        P(),
        P("line", gate, None),
        P("line", gate),
        P("cable", gate),
    )
    return jax.shard_map(
        on_device,
        mesh=split,
        in_specs=placed,
        out_specs=P(gate, "line", "cable"),
        check_vma=False,
    )
```

```python
import jax
import jax.numpy as jnp
from jax import lax
from jax.experimental import pallas as pl
from jax.experimental.pallas import tpu as pltpu
from jax.sharding import Mesh, PartitionSpec as P

NT = 512
LINES = 8
CABLES = 8
GATES = 8
CHIPS_X = 4
OWNERS = CABLES * GATES
PER_DEV = 2048
SHOT_DEV = 4
REC_DEV = 128
APT_DEV = 16
REC_BITS = 10
CAP = 64
HALF = CAP // 2
WIDTH = NT // LINES
LANES = 128
SHARES = LINES * 2
UPPER = 4
TAP = 16
TILE = 256
MOVED = 1024

bf16 = jnp.bfloat16
f32 = jnp.float32
i32 = jnp.int32


def iota(shape, dim):
    return lax.broadcasted_iota(i32, shape, dim)


def params(mib):
    return pltpu.CompilerParams(vmem_limit_bytes=mib * 1024 * 1024)


def owner_of(order):
    aperture = order >> REC_BITS
    receiver = order & ((1 << REC_BITS) - 1)
    return (receiver >> 7) * GATES + (aperture >> 4)


def earlier_matrix():
    return (iota((TILE, TILE), 0) < iota((TILE, TILE), 1)).astype(f32).astype(bf16)


def picked_rows(code_ref, source_ref, out_ref, finish):
    depth = source_ref.shape[0]
    rows = out_ref.shape[0]
    want = iota((TILE, TILE), 0).astype(f32).astype(bf16)

    def tile(m, carry):
        base = pl.multiple_of(m * MOVED, MOVED)
        total = jnp.zeros((MOVED, LANES), f32)
        for c in range(depth // TILE):
            at = slice(c * TILE, (c + 1) * TILE)
            blocks = []
            for b in range(MOVED // TILE):
                code = code_ref[:, at] - (base + b * TILE)
                code = jnp.where((code >= 0) & (code < TILE), code, -1)
                code = code.astype(f32).astype(bf16)
                blocks.append(jnp.where(want == code, bf16(1), bf16(0)))
            total += jnp.dot(
                jnp.concatenate(blocks, axis=0), source_ref[at, :], preferred_element_type=f32
            )
        out_ref[pl.ds(base, MOVED), :] = finish(total, base).astype(out_ref.dtype)
        return carry

    lax.fori_loop(0, rows // MOVED, tile, 0)


def send_kernel(line_ref, me_ref, order_hbm, rec_hbm, out_ref, order_ref, rec_ref, source, code, sems):
    line, me = line_ref[0], me_ref[0]
    order_copy = pltpu.make_async_copy(
        order_hbm.at[pl.ds(pl.multiple_of(me * PER_DEV, PER_DEV), PER_DEV)], order_ref, sems.at[0]
    )
    rec_copy = pltpu.make_async_copy(
        rec_hbm.at[:, pl.ds(pl.multiple_of((line >> 1) * LANES, LANES), LANES)],
        rec_ref,
        sems.at[1],
    )
    order_copy.start()
    rec_copy.start()
    order_copy.wait()
    owner = owner_of(order_ref[...].reshape(1, PER_DEV))
    before = earlier_matrix()
    carry = jnp.zeros((OWNERS, 1), f32)
    for c in range(PER_DEV // TILE):
        lanes = slice(c * TILE, (c + 1) * TILE)
        own = owner[:, lanes]
        onehot = jnp.where(iota((OWNERS, TILE), 0) == own, 1.0, 0.0).astype(f32)
        count = jnp.dot(onehot.astype(bf16), before, preferred_element_type=f32) + carry
        rank = jnp.sum(onehot * count, axis=0, keepdims=True).astype(i32)
        carry = carry + jnp.sum(onehot, axis=1, keepdims=True)
        slot = own * HALF + rank
        code[:, c * TILE : (c + 1) * TILE] = jnp.where(rank < HALF, slot, -1)
        code[:, PER_DEV + c * TILE : PER_DEV + (c + 1) * TILE] = jnp.where(
            rank >= HALF, slot - HALF, -1
        )
    rec_copy.wait()
    odd = line & 1 == 1
    for c in range(PER_DEV // TILE):
        rows = slice(c * TILE, (c + 1) * TILE)
        here = rec_ref[rows, :].astype(f32)
        turned = pltpu.roll(here, WIDTH, 1)
        low = iota((TILE, LANES), 1) < WIDTH
        source[rows, :] = jnp.where(low, jnp.where(odd, turned, here), 0.0).astype(bf16)
        source[PER_DEV + c * TILE : PER_DEV + (c + 1) * TILE, :] = jnp.where(
            low, 0.0, jnp.where(odd, here, turned)
        ).astype(bf16)
    picked_rows(code, source, out_ref, lambda total, base: total)


def send(recorded, trace_order, line, me):
    return pl.pallas_call(
        send_kernel,
        out_shape=jax.ShapeDtypeStruct((OWNERS * HALF, LANES), bf16),
        in_specs=[
            pl.BlockSpec(memory_space=pltpu.SMEM),
            pl.BlockSpec(memory_space=pltpu.SMEM),
            pl.BlockSpec(memory_space=pltpu.HBM),
            pl.BlockSpec(memory_space=pltpu.HBM),
        ],
        out_specs=pl.BlockSpec(memory_space=pltpu.VMEM),
        scratch_shapes=[
            pltpu.VMEM((PER_DEV,), i32),
            pltpu.VMEM((PER_DEV, LANES), bf16),
            pltpu.VMEM((2 * PER_DEV, LANES), bf16),
            pltpu.VMEM((1, 2 * PER_DEV), i32),
            pltpu.SemaphoreType.DMA((2,)),
        ],
        compiler_params=params(58),
        name="send_rows",
    )(line, me, trace_order, recorded)


def place_kernel(me_ref, order_ref, out_ref, held):
    me = me_ref[0]
    before = earlier_matrix()
    carry = jnp.zeros((OWNERS, 1), f32)
    for c in range(PER_DEV // TILE):
        lanes = slice(c * TILE, (c + 1) * TILE)
        order = order_ref[:, lanes]
        mine = owner_of(order) == me
        ones = jnp.where(mine, 1.0, 0.0).astype(f32)
        count = jnp.dot(ones.astype(bf16), before, preferred_element_type=f32) + carry
        carry = carry + jnp.sum(ones, axis=1, keepdims=True)
        distance = iota((OWNERS, TILE), 1) + c * TILE - count.astype(i32)
        receiver = order & (REC_DEV - 1)
        share, rho = receiver & (SHARES - 1), receiver >> 4
        code = share * 64 + (rho & (UPPER - 1)) * APT_DEV + ((order >> REC_BITS) & 15)
        code = code + (rho >> 2) * 1024 + 1
        held[:, lanes] = jnp.where(mine, code * PER_DEV + distance, 0)

    lane = iota((8, LANES), 1)
    row = iota((8, LANES), 0)
    columns = PER_DEV // LANES
    none = jnp.zeros((8, LANES), i32)

    def group(g, carry):
        rows = pl.ds(pl.multiple_of(g * 8, 8), 8)
        kept = [held[rows, c * LANES : (c + 1) * LANES] for c in range(columns)]
        for bit in range(11):
            step = 1 << bit
            if step < LANES:
                turned = [pltpu.roll(v, LANES - step, 1) for v in kept] + [none]
                coming = [
                    jnp.where(lane < LANES - step, turned[c], turned[c + 1])
                    for c in range(columns)
                ]
            else:
                skip = step // LANES
                coming = kept[skip:] + [none] * skip
            kept = [
                jnp.where((new & step) != 0, new, jnp.where((old & step) != 0, 0, old))
                for new, old in zip(coming, kept)
            ]
        slots = kept[0]
        for half in range(2):
            spread = none
            for r in range(4):
                shift = (32 * r - 32 * half) % LANES
                turned = pltpu.roll(slots, shift, 1) if shift else slots
                spread = jnp.where(((row & 3) == r) & ((lane >> 5) == r), turned, spread)
            field = spread >> 11
            for upper in range(2):
                want = (field > 1024 * upper) & (field <= 1024 * upper + 1024)
                value = jnp.where(want, field - 1024 * upper, 0).astype(f32)
                for part in range(2):
                    placed = jnp.sum(value[4 * part : 4 * part + 4], axis=0, keepdims=True)
                    at = pl.ds(pl.multiple_of((2 * g + part) * LANES, LANES), LANES)
                    v = 2 * upper + half
                    out_ref[v : v + 1, at] = placed.astype(i32) - 1
        return carry

    lax.fori_loop(0, OWNERS // 8, group, 0, unroll=4)


def place(orders, me):
    return pl.pallas_call(
        place_kernel,
        out_shape=jax.ShapeDtypeStruct((4, OWNERS * HALF), i32),
        in_specs=[
            pl.BlockSpec(memory_space=pltpu.SMEM),
            pl.BlockSpec(memory_space=pltpu.VMEM),
        ],
        out_specs=pl.BlockSpec(memory_space=pltpu.VMEM),
        scratch_shapes=[pltpu.VMEM((OWNERS, PER_DEV), i32)],
        compiler_params=params(12),
        cost_estimate=pl.CostEstimate(
            flops=4 * 2**30, bytes_accessed=2**20, transcendentals=0
        ),
        name="place_rows",
    )(me, orders)


def receive_kernel(key_ref, got_ref, mask_ref, out_ref, source, code):
    for v in range(4):
        code[:, v * PER_DEV : (v + 1) * PER_DEV] = key_ref[v : v + 1, :]
    for c in range(PER_DEV // TILE):
        rows = slice(c * TILE, (c + 1) * TILE)
        here = got_ref[rows, :].astype(f32)
        turned = pltpu.roll(here, WIDTH, 1)
        low = iota((TILE, LANES), 1) < WIDTH
        parts = (
            jnp.where(low, here, 0.0),
            jnp.where(low, turned, 0.0),
            jnp.where(low, 0.0, turned),
            jnp.where(low, 0.0, here),
        )
        for v, part in enumerate(parts):
            source[v * PER_DEV + c * TILE : v * PER_DEV + (c + 1) * TILE, :] = part.astype(bf16)

    def weighted(total, base):
        return total * mask_ref[pl.ds(base, MOVED), :].astype(f32)

    picked_rows(code, source, out_ref, weighted)


def receive(keys, got, weights):
    return pl.pallas_call(
        receive_kernel,
        out_shape=jax.ShapeDtypeStruct((SHARES * 64, LANES), bf16),
        in_specs=[pl.BlockSpec(memory_space=pltpu.VMEM)] * 3,
        out_specs=pl.BlockSpec(memory_space=pltpu.VMEM),
        scratch_shapes=[
            pltpu.VMEM((4 * PER_DEV, LANES), bf16),
            pltpu.VMEM((1, 4 * PER_DEV), i32),
        ],
        compiler_params=params(12),
        name="receive_rows",
    )(keys, got, weights)


def near_kernel(where_ref, own_ref, other_ref, near_ref):
    me, core = where_ref[0], where_ref[1]

    def held(line):
        offset = line ^ me
        return ((offset & 1) << 2) | (offset & 2) | (offset >> 2)

    def one_line(line, carry):
        here = held(line)
        before = held(jnp.maximum(line - 1, 0))
        after = held(jnp.minimum(line + 1, LINES - 1))
        for side, all_ref in enumerate((own_ref, other_ref)):
            at = pl.multiple_of((core ^ side) * 256, 256)
            pick = all_ref[here, 128:144, :]
            first, own = pick == bf16(0), pick == bf16(1)
            for g in range(8):
                rows = slice(g * 16, (g + 1) * 16)
                near_ref[line, rows, pl.ds(at, 256)] = jnp.where(
                    first,
                    all_ref[before, rows, :],
                    jnp.where(own, all_ref[here, rows, :], all_ref[after, rows, :]),
                )
        return carry

    lax.fori_loop(0, LINES, one_line, 0)


def near(where, own, other):
    return pl.pallas_call(
        near_kernel,
        out_shape=jax.ShapeDtypeStruct((LINES, 128, 512), bf16),
        in_specs=[
            pl.BlockSpec(memory_space=pltpu.SMEM),
            pl.BlockSpec(memory_space=pltpu.VMEM),
            pl.BlockSpec(memory_space=pltpu.VMEM),
        ],
        out_specs=pl.BlockSpec(memory_space=pltpu.VMEM),
        compiler_params=params(8),
        name="near_rows",
    )(where, own, other)


def swapped(held, axis, bit):
    size = lax.axis_size(axis)
    return lax.ppermute(held, axis, [(i, i ^ bit) for i in range(size)])


def lag_rows(gather_ref, base, lagged):
    low = iota((APT_DEV, LANES), 1) < WIDTH
    lane = iota((TAP, LANES), 1)
    tap = iota((TAP, LANES), 0)

    def one_block(n, carry):
        core = n // UPPER
        rho = n % UPPER
        for c in range(4):
            rows = pl.ds(pl.multiple_of(rho * 16, 16), 16)
            even = gather_ref[4 * c + core, rows, :].astype(f32)
            odd = gather_ref[4 * c + 2 + core, rows, :].astype(f32)
            base[0, :, c * LANES : (c + 1) * LANES] = jnp.where(
                low, even, pltpu.roll(odd, WIDTH, 1)
            )
            base[1, :, c * LANES : (c + 1) * LANES] = jnp.where(
                low, pltpu.roll(even, WIDTH, 1), odd
            )
        for upper in range(2):
            lanes = pl.ds(pl.multiple_of((2 * rho + upper) * LANES, LANES), LANES)
            for x in range(APT_DEV):
                rows = pl.ds(pl.multiple_of((core * APT_DEV + x) * TAP, TAP), TAP)
                last = jnp.zeros((TAP, LANES), f32)
                for c in range(4):
                    row = base[upper, x : x + 1, c * LANES : (c + 1) * LANES]
                    row = jnp.broadcast_to(row, (TAP, LANES))
                    turned = pltpu.roll(row, 0, 1, stride=1, stride_axis=0)
                    lagged[c, rows, lanes] = jnp.where(lane >= tap, turned, last).astype(bf16)
                    last = turned
        return carry

    lax.fori_loop(0, 2 * UPPER, one_block, 0)


def sum_lines(near_ref, lagged, out_ref):
    lane = iota((8 * LINES, LANES), 1)
    low = lane < WIDTH

    for rho in range(UPPER):
        spill = [jnp.zeros((8 * LINES, LANES), f32)] * 2
        before = [jnp.zeros((8 * LINES, LANES), f32)] * 2
        for i in range(4):
            total = None
            for d in range(i + 1):
                here = near_ref[:, 32 * (i - d) : 32 * (i - d) + 32, :].reshape(32 * LINES, 512)
                part = jnp.dot(
                    here, lagged[d, :, 256 * rho : 256 * rho + 256], preferred_element_type=f32
                )
                total = part if total is None else total + part
            total = total.reshape(LINES, 4, 8, 256)
            done = []
            for upper in range(2):
                current = spill[upper]
                later = jnp.zeros((8 * LINES, LANES), f32)
                for q in range(4):
                    piece = total[:, q, :, upper * LANES : (upper + 1) * LANES]
                    piece = piece.reshape(8 * LINES, LANES)
                    if q == 0:
                        current = current + piece
                    else:
                        turned = pltpu.roll(piece, 32 * q, 1)
                        current = current + jnp.where(lane >= 32 * q, turned, 0.0)
                        later = later + jnp.where(lane >= 32 * q, 0.0, turned)
                turned = pltpu.roll(current, TAP, 1)
                moved = jnp.where(lane >= TAP, turned, before[upper])
                spill[upper] = later
                before[upper] = turned
                both = current.reshape(LINES, 8, LANES)[:, 0:4] + moved.reshape(LINES, 8, LANES)[:, 4:8]
                done.append(both.reshape(4 * LINES, LANES))
            one, two = done
            half = low[: 4 * LINES]
            rows = slice(4 * rho, 4 * rho + 4)
            even = jnp.where(half, one, pltpu.roll(two, WIDTH, 1)).reshape(LINES, 4, LANES)
            odd = jnp.where(half, pltpu.roll(one, WIDTH, 1), two).reshape(LINES, 4, LANES)
            out_ref[:, 2 * i, rows, :] = even
            out_ref[:, 2 * i + 1, rows, :] = odd


def predict_kernel(gather_ref, near_ref, out_ref, base, lagged):
    lag_rows(gather_ref, base, lagged)
    sum_lines(near_ref, lagged, out_ref)


def predict(gathers, near_all):
    return pl.pallas_call(
        predict_kernel,
        out_shape=jax.ShapeDtypeStruct((LINES, GATES, 4 * UPPER, LANES), f32),
        in_specs=[pl.BlockSpec(memory_space=pltpu.VMEM)] * 2,
        out_specs=pl.BlockSpec(memory_space=pltpu.VMEM),
        scratch_shapes=[
            pltpu.VMEM((2, APT_DEV, NT), f32),
            pltpu.VMEM((4, 2 * APT_DEV * TAP, 2 * UPPER * LANES), bf16),
        ],
        compiler_params=params(20),
        name="predict_part",
    )(gathers, near_all)


def finish_kernel(parts_ref, out_ref):
    total = jnp.sum(parts_ref[...], axis=1).reshape(SHARES, 4 * UPPER, LANES)
    shots = []
    for s in range(SHOT_DEV):
        rows = []
        for rho in range(UPPER):
            rows.append(total[:, 4 * rho + s, :])
        turned = jnp.transpose(jnp.concatenate(rows, axis=0))
        shots.append(jnp.concatenate([turned[:WIDTH], turned[WIDTH:]], axis=1))
    out_ref[...] = jnp.stack(shots, axis=1).astype(out_ref.dtype)


def finish(parts):
    return pl.pallas_call(
        finish_kernel,
        out_shape=jax.ShapeDtypeStruct((NT // GATES, SHOT_DEV, REC_DEV), bf16),
        in_specs=[pl.BlockSpec(memory_space=pltpu.VMEM)],
        out_specs=pl.BlockSpec(memory_space=pltpu.VMEM),
        compiler_params=params(6),
        name="finish_sum",
    )(parts)


def on_device(recorded, trace_order, shot_traces, line_picks, aperture_mask):
    gate = ("gx", "core")
    me = lax.axis_index(("cable",) + gate).astype(i32)
    line = lax.axis_index("line").astype(i32)

    spare = ((0, 0), (0, 0), (0, LANES - 1))
    joined = jnp.concatenate(
        [shot_traces, jnp.pad(line_picks.astype(bf16)[:, :, None], spare)], axis=2
    )
    far = swapped(joined, "line", 4)

    outgoing = send(recorded, trace_order, line.reshape(1), me.reshape(1))
    got = lax.all_to_all(
        outgoing.reshape(OWNERS, HALF, LANES),
        ("cable",) + gate,
        split_axis=0,
        concat_axis=0,
        tiled=True,
    )
    late, joined, far, trace_order, aperture_mask = lax.optimization_barrier(
        (outgoing, joined, far, trace_order, aperture_mask)
    )
    both = jnp.stack([joined, far])
    shots = both[:, :, :, :NT].reshape(2, SHOT_DEV, APT_DEV, NT // TAP, TAP)
    shots = jnp.transpose(shots, (0, 3, 1, 2, 4)).reshape(2, NT // TAP * SHOT_DEV, APT_DEV * TAP)
    picks = jnp.tile(jnp.repeat(both[:, :, :, NT], TAP, axis=2), (1, 4, 1))
    held = jnp.concatenate([shots, picks], axis=1)
    two = swapped(held, "line", 2)
    keys = place(trace_order.reshape(OWNERS, PER_DEV), me.reshape(1))
    keys, two = lax.optimization_barrier((keys, two))
    held = jnp.concatenate([held, two], axis=0)
    one = swapped(held, "line", 1)
    weights = aperture_mask.astype(bf16).reshape(2, UPPER, SHARES, APT_DEV)
    weights = jnp.transpose(weights, (2, 1, 3, 0)).reshape(SHARES * 64, 2)
    weights = jnp.repeat(weights, WIDTH, axis=1)
    mine = receive(keys, got.reshape(OWNERS * HALF, LANES), weights)
    gathers = lax.all_to_all(
        mine.reshape(SHARES, 64, LANES), ("line", "core"), split_axis=0, concat_axis=0, tiled=True
    )
    late, one = lax.optimization_barrier((mine, one))
    own = jnp.concatenate([held, one], axis=0)
    other = swapped(own, "core", 1)
    near_all = near(jnp.stack([line, lax.axis_index("core").astype(i32)]), own, other)
    part = predict(gathers, near_all)
    parts = lax.all_to_all(
        part.reshape(OWNERS, 4 * UPPER, LANES), ("line",) + gate, split_axis=0, concat_axis=0, tiled=True)
    return finish(parts.reshape(LINES, CHIPS_X, 2, 4 * UPPER, LANES))


def solution(mesh):
    split = Mesh(mesh.devices.reshape(LINES, CABLES, CHIPS_X, 2), ("line", "cable", "gx", "core"))
    gate = ("gx", "core")
    placed = (
        P(("cable",) + gate, None),
        P(),
        P("line", gate, None),
        P("line", gate),
        P("cable", gate),
    )
    return jax.shard_map(
        on_device,
        mesh=split,
        in_specs=placed,
        out_specs=P(gate, "line", "cable"),
        check_vma=False,
    )
```

```python
import jax
import jax.numpy as jnp
from jax import lax
from jax.experimental import pallas as pl
from jax.experimental.pallas import tpu as pltpu
from jax.sharding import Mesh, PartitionSpec as P

NT = 512
LINES = 8
CABLES = 8
GATES = 8
CHIPS_X = 4
OWNERS = CABLES * GATES
PER_DEV = 2048
SHOT_DEV = 4
REC_DEV = 128
APT_DEV = 16
REC_BITS = 10
CAP = 64
HALF = CAP // 2
WIDTH = NT // LINES
LANES = 128
SHARES = LINES * 2
UPPER = 4
TAP = 16
TILE = 256
MOVED = 1024

bf16 = jnp.bfloat16
f32 = jnp.float32
i32 = jnp.int32


def iota(shape, dim):
    return lax.broadcasted_iota(i32, shape, dim)


def params(mib):
    return pltpu.CompilerParams(vmem_limit_bytes=mib * 1024 * 1024)


def owner_of(order):
    aperture = order >> REC_BITS
    receiver = order & ((1 << REC_BITS) - 1)
    return (receiver >> 7) * GATES + (aperture >> 4)


def earlier_matrix():
    return (iota((TILE, TILE), 0) < iota((TILE, TILE), 1)).astype(f32).astype(bf16)


def picked_rows(code_ref, source_ref, out_ref, finish):
    depth = source_ref.shape[0]
    rows = out_ref.shape[0]
    want = iota((TILE, TILE), 0).astype(f32).astype(bf16)

    def tile(m, carry):
        base = pl.multiple_of(m * MOVED, MOVED)
        total = jnp.zeros((MOVED, LANES), f32)
        for c in range(depth // TILE):
            at = slice(c * TILE, (c + 1) * TILE)
            blocks = []
            for b in range(MOVED // TILE):
                code = code_ref[:, at] - (base + b * TILE)
                code = jnp.where((code >= 0) & (code < TILE), code, -1)
                code = code.astype(f32).astype(bf16)
                blocks.append(jnp.where(want == code, bf16(1), bf16(0)))
            total += jnp.dot(
                jnp.concatenate(blocks, axis=0), source_ref[at, :], preferred_element_type=f32
            )
        out_ref[pl.ds(base, MOVED), :] = finish(total, base).astype(out_ref.dtype)
        return carry

    lax.fori_loop(0, rows // MOVED, tile, 0)


def send_kernel(line_ref, me_ref, order_hbm, rec_hbm, out_ref, order_ref, rec_ref, source, code, sems):
    line, me = line_ref[0], me_ref[0]
    order_copy = pltpu.make_async_copy(
        order_hbm.at[pl.ds(pl.multiple_of(me * PER_DEV, PER_DEV), PER_DEV)], order_ref, sems.at[0]
    )
    rec_copy = pltpu.make_async_copy(
        rec_hbm.at[:, pl.ds(pl.multiple_of((line >> 1) * LANES, LANES), LANES)],
        rec_ref,
        sems.at[1],
    )
    order_copy.start()
    rec_copy.start()
    order_copy.wait()
    owner = owner_of(order_ref[...].reshape(1, PER_DEV))
    before = earlier_matrix()
    carry = jnp.zeros((OWNERS, 1), f32)
    for c in range(PER_DEV // TILE):
        lanes = slice(c * TILE, (c + 1) * TILE)
        own = owner[:, lanes]
        onehot = jnp.where(iota((OWNERS, TILE), 0) == own, 1.0, 0.0).astype(f32)
        count = jnp.dot(onehot.astype(bf16), before, preferred_element_type=f32) + carry
        rank = jnp.sum(onehot * count, axis=0, keepdims=True).astype(i32)
        carry = carry + jnp.sum(onehot, axis=1, keepdims=True)
        slot = own * HALF + rank
        code[:, c * TILE : (c + 1) * TILE] = jnp.where(rank < HALF, slot, -1)
        code[:, PER_DEV + c * TILE : PER_DEV + (c + 1) * TILE] = jnp.where(
            rank >= HALF, slot - HALF, -1
        )
    rec_copy.wait()
    odd = line & 1 == 1
    for c in range(PER_DEV // TILE):
        rows = slice(c * TILE, (c + 1) * TILE)
        here = rec_ref[rows, :].astype(f32)
        turned = pltpu.roll(here, WIDTH, 1)
        low = iota((TILE, LANES), 1) < WIDTH
        source[rows, :] = jnp.where(low, jnp.where(odd, turned, here), 0.0).astype(bf16)
        source[PER_DEV + c * TILE : PER_DEV + (c + 1) * TILE, :] = jnp.where(
            low, 0.0, jnp.where(odd, here, turned)
        ).astype(bf16)
    picked_rows(code, source, out_ref, lambda total, base: total)


def send(recorded, trace_order, line, me):
    return pl.pallas_call(
        send_kernel,
        out_shape=jax.ShapeDtypeStruct((OWNERS * HALF, LANES), bf16),
        in_specs=[
            pl.BlockSpec(memory_space=pltpu.SMEM),
            pl.BlockSpec(memory_space=pltpu.SMEM),
            pl.BlockSpec(memory_space=pltpu.HBM),
            pl.BlockSpec(memory_space=pltpu.HBM),
        ],
        out_specs=pl.BlockSpec(memory_space=pltpu.VMEM),
        scratch_shapes=[
            pltpu.VMEM((PER_DEV,), i32),
            pltpu.VMEM((PER_DEV, LANES), bf16),
            pltpu.VMEM((2 * PER_DEV, LANES), bf16),
            pltpu.VMEM((1, 2 * PER_DEV), i32),
            pltpu.SemaphoreType.DMA((2,)),
        ],
        compiler_params=params(58),
        name="send_rows",
    )(line, me, trace_order, recorded)


def place_kernel(me_ref, order_ref, out_ref, held):
    me = me_ref[0]
    before = earlier_matrix()
    carry = jnp.zeros((OWNERS, 1), f32)
    for c in range(PER_DEV // TILE):
        lanes = slice(c * TILE, (c + 1) * TILE)
        order = order_ref[:, lanes]
        mine = owner_of(order) == me
        ones = jnp.where(mine, 1.0, 0.0).astype(f32)
        count = jnp.dot(ones.astype(bf16), before, preferred_element_type=f32) + carry
        carry = carry + jnp.sum(ones, axis=1, keepdims=True)
        distance = iota((OWNERS, TILE), 1) + c * TILE - count.astype(i32)
        receiver = order & (REC_DEV - 1)
        share, rho = receiver & (SHARES - 1), receiver >> 4
        code = share * 64 + (rho & (UPPER - 1)) * APT_DEV + ((order >> REC_BITS) & 15)
        code = code + (rho >> 2) * 1024 + 1
        held[:, lanes] = jnp.where(mine, code * PER_DEV + distance, 0)

    lane = iota((8, LANES), 1)
    row = iota((8, LANES), 0)
    columns = PER_DEV // LANES
    none = jnp.zeros((8, LANES), i32)

    def group(g, carry):
        rows = pl.ds(pl.multiple_of(g * 8, 8), 8)
        kept = [held[rows, c * LANES : (c + 1) * LANES] for c in range(columns)]
        for bit in range(11):
            step = 1 << bit
            if step < LANES:
                turned = [pltpu.roll(v, LANES - step, 1) for v in kept] + [none]
                coming = [
                    jnp.where(lane < LANES - step, turned[c], turned[c + 1])
                    for c in range(columns)
                ]
            else:
                skip = step // LANES
                coming = kept[skip:] + [none] * skip
            kept = [
                jnp.where((new & step) != 0, new, jnp.where((old & step) != 0, 0, old))
                for new, old in zip(coming, kept)
            ]
        slots = kept[0]
        for half in range(2):
            spread = none
            for r in range(4):
                shift = (32 * r - 32 * half) % LANES
                turned = pltpu.roll(slots, shift, 1) if shift else slots
                spread = jnp.where(((row & 3) == r) & ((lane >> 5) == r), turned, spread)
            field = spread >> 11
            for upper in range(2):
                want = (field > 1024 * upper) & (field <= 1024 * upper + 1024)
                value = jnp.where(want, field - 1024 * upper, 0).astype(f32)
                for part in range(2):
                    placed = jnp.sum(value[4 * part : 4 * part + 4], axis=0, keepdims=True)
                    at = pl.ds(pl.multiple_of((2 * g + part) * LANES, LANES), LANES)
                    v = 2 * upper + half
                    out_ref[v : v + 1, at] = placed.astype(i32) - 1
        return carry

    lax.fori_loop(0, OWNERS // 8, group, 0, unroll=4)


def place(orders, me):
    return pl.pallas_call(
        place_kernel,
        out_shape=jax.ShapeDtypeStruct((4, OWNERS * HALF), i32),
        in_specs=[
            pl.BlockSpec(memory_space=pltpu.SMEM),
            pl.BlockSpec(memory_space=pltpu.VMEM),
        ],
        out_specs=pl.BlockSpec(memory_space=pltpu.VMEM),
        scratch_shapes=[pltpu.VMEM((OWNERS, PER_DEV), i32)],
        compiler_params=params(12),
        cost_estimate=pl.CostEstimate(
            flops=4 * 2**30, bytes_accessed=2**20, transcendentals=0
        ),
        name="place_rows",
    )(me, orders)


def receive_kernel(key_ref, got_ref, mask_ref, out_ref, source, code):
    for v in range(4):
        code[:, v * PER_DEV : (v + 1) * PER_DEV] = key_ref[v : v + 1, :]
    for c in range(PER_DEV // TILE):
        rows = slice(c * TILE, (c + 1) * TILE)
        here = got_ref[rows, :].astype(f32)
        turned = pltpu.roll(here, WIDTH, 1)
        low = iota((TILE, LANES), 1) < WIDTH
        parts = (
            jnp.where(low, here, 0.0),
            jnp.where(low, turned, 0.0),
            jnp.where(low, 0.0, turned),
            jnp.where(low, 0.0, here),
        )
        for v, part in enumerate(parts):
            source[v * PER_DEV + c * TILE : v * PER_DEV + (c + 1) * TILE, :] = part.astype(bf16)

    def weighted(total, base):
        return total * mask_ref[pl.ds(base, MOVED), :].astype(f32)

    picked_rows(code, source, out_ref, weighted)


def receive(keys, got, weights):
    return pl.pallas_call(
        receive_kernel,
        out_shape=jax.ShapeDtypeStruct((SHARES * 64, LANES), bf16),
        in_specs=[pl.BlockSpec(memory_space=pltpu.VMEM)] * 3,
        out_specs=pl.BlockSpec(memory_space=pltpu.VMEM),
        scratch_shapes=[
            pltpu.VMEM((4 * PER_DEV, LANES), bf16),
            pltpu.VMEM((1, 4 * PER_DEV), i32),
        ],
        compiler_params=params(12),
        name="receive_rows",
    )(keys, got, weights)


def near_kernel(where_ref, own_ref, other_ref, near_ref):
    me, core = where_ref[0], where_ref[1]

    def held(line):
        offset = line ^ me
        return ((offset & 1) << 2) | (offset & 2) | (offset >> 2)

    def one_line(line, carry):
        here = held(line)
        before = held(jnp.maximum(line - 1, 0))
        after = held(jnp.minimum(line + 1, LINES - 1))
        for side, all_ref in enumerate((own_ref, other_ref)):
            at = pl.multiple_of((core ^ side) * 256, 256)
            pick = all_ref[here, 128:144, :]
            first, own = pick == bf16(0), pick == bf16(1)
            for g in range(8):
                rows = slice(g * 16, (g + 1) * 16)
                near_ref[line, rows, pl.ds(at, 256)] = jnp.where(
                    first,
                    all_ref[before, rows, :],
                    jnp.where(own, all_ref[here, rows, :], all_ref[after, rows, :]),
                )
        return carry

    lax.fori_loop(0, LINES, one_line, 0)


def near(where, own, other):
    return pl.pallas_call(
        near_kernel,
        out_shape=jax.ShapeDtypeStruct((LINES, 128, 512), bf16),
        in_specs=[
            pl.BlockSpec(memory_space=pltpu.SMEM),
            pl.BlockSpec(memory_space=pltpu.VMEM),
            pl.BlockSpec(memory_space=pltpu.VMEM),
        ],
        out_specs=pl.BlockSpec(memory_space=pltpu.VMEM),
        compiler_params=params(8),
        name="near_rows",
    )(where, own, other)


def swapped(held, axis, bit):
    size = lax.axis_size(axis)
    return lax.ppermute(held, axis, [(i, i ^ bit) for i in range(size)])


def lag_rows(gather_ref, base, lagged):
    low = iota((APT_DEV, LANES), 1) < WIDTH
    lane = iota((TAP, LANES), 1)
    tap = iota((TAP, LANES), 0)

    def one_block(n, carry):
        core = n // UPPER
        rho = n % UPPER
        for c in range(4):
            rows = pl.ds(pl.multiple_of(rho * 16, 16), 16)
            even = gather_ref[4 * c + core, rows, :].astype(f32)
            odd = gather_ref[4 * c + 2 + core, rows, :].astype(f32)
            base[0, :, c * LANES : (c + 1) * LANES] = jnp.where(
                low, even, pltpu.roll(odd, WIDTH, 1)
            )
            base[1, :, c * LANES : (c + 1) * LANES] = jnp.where(
                low, pltpu.roll(even, WIDTH, 1), odd
            )
        for upper in range(2):
            lanes = pl.ds(pl.multiple_of((2 * rho + upper) * LANES, LANES), LANES)
            for x in range(APT_DEV):
                rows = pl.ds(pl.multiple_of((core * APT_DEV + x) * TAP, TAP), TAP)
                last = jnp.zeros((TAP, LANES), f32)
                for c in range(4):
                    row = base[upper, x : x + 1, c * LANES : (c + 1) * LANES]
                    row = jnp.broadcast_to(row, (TAP, LANES))
                    turned = pltpu.roll(row, 0, 1, stride=1, stride_axis=0)
                    lagged[c, rows, lanes] = jnp.where(lane >= tap, turned, last).astype(bf16)
                    last = turned
        return carry

    lax.fori_loop(0, 2 * UPPER, one_block, 0)


def sum_lines(near_ref, lagged, out_ref):
    lane = iota((8 * LINES, LANES), 1)
    low = lane < WIDTH

    for rho in range(UPPER):
        spill = [jnp.zeros((8 * LINES, LANES), f32)] * 2
        before = [jnp.zeros((8 * LINES, LANES), f32)] * 2
        for i in range(4):
            total = None
            for d in range(i + 1):
                here = near_ref[:, 32 * (i - d) : 32 * (i - d) + 32, :].reshape(32 * LINES, 512)
                part = jnp.dot(
                    here, lagged[d, :, 256 * rho : 256 * rho + 256], preferred_element_type=f32
                )
                total = part if total is None else total + part
            total = total.reshape(LINES, 4, 8, 256)
            done = []
            for upper in range(2):
                current = spill[upper]
                later = jnp.zeros((8 * LINES, LANES), f32)
                for q in range(4):
                    piece = total[:, q, :, upper * LANES : (upper + 1) * LANES]
                    piece = piece.reshape(8 * LINES, LANES)
                    if q == 0:
                        current = current + piece
                    else:
                        turned = pltpu.roll(piece, 32 * q, 1)
                        current = current + jnp.where(lane >= 32 * q, turned, 0.0)
                        later = later + jnp.where(lane >= 32 * q, 0.0, turned)
                turned = pltpu.roll(current, TAP, 1)
                moved = jnp.where(lane >= TAP, turned, before[upper])
                spill[upper] = later
                before[upper] = turned
                both = current.reshape(LINES, 8, LANES)[:, 0:4] + moved.reshape(LINES, 8, LANES)[:, 4:8]
                done.append(both.reshape(4 * LINES, LANES))
            one, two = done
            half = low[: 4 * LINES]
            rows = slice(4 * rho, 4 * rho + 4)
            even = jnp.where(half, one, pltpu.roll(two, WIDTH, 1)).reshape(LINES, 4, LANES)
            odd = jnp.where(half, pltpu.roll(one, WIDTH, 1), two).reshape(LINES, 4, LANES)
            out_ref[:, 2 * i, rows, :] = even
            out_ref[:, 2 * i + 1, rows, :] = odd


def predict_kernel(gather_ref, near_ref, out_ref, base, lagged):
    lag_rows(gather_ref, base, lagged)
    sum_lines(near_ref, lagged, out_ref)


def predict(gathers, near_all):
    return pl.pallas_call(
        predict_kernel,
        out_shape=jax.ShapeDtypeStruct((LINES, GATES, 4 * UPPER, LANES), f32),
        in_specs=[pl.BlockSpec(memory_space=pltpu.VMEM)] * 2,
        out_specs=pl.BlockSpec(memory_space=pltpu.VMEM),
        scratch_shapes=[
            pltpu.VMEM((2, APT_DEV, NT), f32),
            pltpu.VMEM((4, 2 * APT_DEV * TAP, 2 * UPPER * LANES), bf16),
        ],
        compiler_params=params(20),
        name="predict_part",
    )(gathers, near_all)


def finish_kernel(parts_ref, out_ref):
    total = jnp.sum(parts_ref[...], axis=1).reshape(SHARES, 4 * UPPER, LANES)
    shots = []
    for s in range(SHOT_DEV):
        rows = []
        for rho in range(UPPER):
            rows.append(total[:, 4 * rho + s, :])
        turned = jnp.transpose(jnp.concatenate(rows, axis=0))
        shots.append(jnp.concatenate([turned[:WIDTH], turned[WIDTH:]], axis=1))
    out_ref[...] = jnp.stack(shots, axis=1).astype(out_ref.dtype)


def finish(parts):
    return pl.pallas_call(
        finish_kernel,
        out_shape=jax.ShapeDtypeStruct((NT // GATES, SHOT_DEV, REC_DEV), bf16),
        in_specs=[pl.BlockSpec(memory_space=pltpu.VMEM)],
        out_specs=pl.BlockSpec(memory_space=pltpu.VMEM),
        compiler_params=params(6),
        name="finish_sum",
    )(parts)


def on_device(recorded, trace_order, shot_traces, line_picks, aperture_mask):
    gate = ("gx", "core")
    me = lax.axis_index(("cable",) + gate).astype(i32)
    line = lax.axis_index("line").astype(i32)

    spare = ((0, 0), (0, 0), (0, LANES - 1))
    joined = jnp.concatenate(
        [shot_traces, jnp.pad(line_picks.astype(bf16)[:, :, None], spare)], axis=2
    )
    far = swapped(joined, "line", 4)
    far, line_at = lax.optimization_barrier((far, line.reshape(1)))

    outgoing = send(recorded, trace_order, line_at, me.reshape(1))
    got = lax.all_to_all(
        outgoing.reshape(OWNERS, HALF, LANES),
        ("cable",) + gate,
        split_axis=0,
        concat_axis=0,
        tiled=True,
    )
    late, joined, far, trace_order, aperture_mask = lax.optimization_barrier(
        (outgoing, joined, far, trace_order, aperture_mask)
    )
    both = jnp.stack([joined, far])
    shots = both[:, :, :, :NT].reshape(2, SHOT_DEV, APT_DEV, NT // TAP, TAP)
    shots = jnp.transpose(shots, (0, 3, 1, 2, 4)).reshape(2, NT // TAP * SHOT_DEV, APT_DEV * TAP)
    picks = jnp.tile(jnp.repeat(both[:, :, :, NT], TAP, axis=2), (1, 4, 1))
    held = jnp.concatenate([shots, picks], axis=1)
    near_by = [swapped(held, "line", bit) for bit in (2, 1, 3)]
    keys = place(trace_order.reshape(OWNERS, PER_DEV), me.reshape(1))
    weights = aperture_mask.astype(bf16).reshape(2, UPPER, SHARES, APT_DEV)
    weights = jnp.transpose(weights, (2, 1, 3, 0)).reshape(SHARES * 64, 2)
    weights = jnp.repeat(weights, WIDTH, axis=1)
    mine = receive(keys, got.reshape(OWNERS * HALF, LANES), weights)
    gathers = lax.all_to_all(
        mine.reshape(SHARES, 64, LANES), ("line", "core"), split_axis=0, concat_axis=0, tiled=True
    )
    late, near_by = lax.optimization_barrier((mine, near_by))
    own = jnp.concatenate([held] + near_by, axis=0)
    other = swapped(own, "core", 1)
    near_all = near(jnp.stack([line, lax.axis_index("core").astype(i32)]), own, other)
    part = predict(gathers, near_all)
    parts = lax.all_to_all(
        part.reshape(OWNERS, 4 * UPPER, LANES), ("line",) + gate, split_axis=0, concat_axis=0, tiled=True)
    return finish(parts.reshape(LINES, CHIPS_X, 2, 4 * UPPER, LANES))


def solution(mesh):
    split = Mesh(mesh.devices.reshape(LINES, CABLES, CHIPS_X, 2), ("line", "cable", "gx", "core"))
    gate = ("gx", "core")
    placed = (
        P(("cable",) + gate, None),
        P(),
        P("line", gate, None),
        P("line", gate),
        P("cable", gate),
    )
    return jax.shard_map(
        on_device,
        mesh=split,
        in_specs=placed,
        out_specs=P(gate, "line", "cable"),
        check_vma=False,
    )
```
